256 devices in a mesh: pipe: 8 (over z), expert: 32 (over y, x, core).
Axes of the slice: x: 4, y: 4, z: 8, core: 2. Of those that a mesh axis runs over, the one named last changes fastest.
Arguments:
- activations: bfloat16 [2, 2048, 2560], P(None, 'expert'), may hold values from -6 to 6
- norm_gain: bfloat16 [8, 2560], P('pipe'), may hold values from 0.099609375 to 1.8984375
- placement: int32 [8, 32], P('pipe'), may hold values from 0 to 31, each once within a row
- expert_ids: int32 [8, 2, 2048, 6], P('pipe', None, 'expert'), may hold values from 0 to 31, all different within a row; in each aligned block of 32 rows (0 to 31, 32 to 63, ..., all dimensions but the last counted through in order) at most 9 rows name the same one
- expert_weights: float32 [8, 2, 2048, 6], P('pipe', None, 'expert'), may hold values from 0.05 to 0.45
- gate_store: bfloat16 [8, 32, 2560, 768], P('pipe', 'expert'), may hold values from -0.125 to 0.125
- up_store: bfloat16 [8, 32, 2560, 768], P('pipe', 'expert'), may hold values from -0.125 to 0.125
- down_store: bfloat16 [8, 32, 768, 2560], P('pipe', 'expert'), may hold values from -0.21875 to 0.21875
Outputs:
- layer_outputs: bfloat16 [8, 2, 2048, 2560], P('pipe', None, 'expert')
The draws below stay inside these ranges and needn't reach their ends.
Inputs may be any that keep to these rules, and one draw needn't show every extreme that they name: `expert_ids`: in every aligned block of 32 rows (rows of all leading dimensions taken in order, so a device's 64 tokens of one layer and microbatch are two blocks) no expert is named by more than 9 rows; some expert is named by exactly 9 rows in some block of every draw. A row names 6 different experts. Each row is a permutation: slot s of layer l holds the weights of expert placement[l, s].
All inputs are finite; a program needn't handle non-finite values.
Results may differ from the reference program's by a relative error of at most 0.024.
Values may be sent and summed in bfloat16 or wider, within the bound.
A program may use at most 64 MiB of HBM per device.

```python
import math
import jax
import jax.numpy as jnp
import numpy as np
from jax import lax

D = 2560
FF = 768
TOPK = 6
MICRO = 2
LAYERS = 8
EXPERTS = 32
TOKENS = 2048
HB = 32
MOSTH = 9


def steps_of(stream_key, extent, pieces, smallest, largest):
    def one(axis_at, shards_of):
        steps = jax.random.uniform(jax.random.fold_in(jax.random.fold_in(stream_key, 6), axis_at), (shards_of,), jnp.float32, smallest / len(pieces), largest / len(pieces))
        return jnp.repeat(jnp.exp(steps), extent[axis_at] // shards_of).reshape((-1,) + (1,) * (len(extent) - axis_at - 1))

    level = one(*pieces[0])
    for cut in pieces[1:]:
        level = level * one(*cut)
    return level


def assign_block(own_key, own, number, rows, number_of, top, reach, lean):
    sequence = jax.random.permutation(own_key, number_of)
    crowded, usual = shares(number_of, rows * top, reach, lean, True), shares(number_of, rows * top, reach, lean, False)
    places = jnp.arange(number_of)

    def named(tallies, offset_by):
        used = int((tallies > 0).sum())
        fixed = max(1, used // 4)
        moved = fixed + (places - fixed + offset_by * (used - fixed)) % max(1, number_of - fixed)
        return jnp.zeros((number_of,), jnp.int32).at[sequence[jnp.where(places < fixed, places, moved)]].set(jnp.asarray(tallies, jnp.int32))

    tallies = jnp.where(number % 4 == 0, named(crowded, number // 4), named(usual, number - number // 4 - 1))
    mixed = jax.random.permutation(jax.random.fold_in(own, 3), number_of)
    source_of, sink = mixed[0:number_of // 2 * 2:2], mixed[1:number_of // 2 * 2:2]
    room = jnp.minimum(tallies[source_of] - 1, reach - tallies[sink]) // 2
    room = jnp.where((source_of == sequence[0]) | (sink == sequence[0]) | (tallies[sink] == 0), 0, jnp.maximum(room, 0))
    moved = jax.random.randint(jax.random.fold_in(own, 4), (number_of // 2,), 0, 1 << 20) % (room + 1)
    tallies = tallies.at[source_of].add(-moved).at[sink].add(moved)
    members = jnp.searchsorted(jnp.cumsum(tallies), jnp.arange(rows * top), side="right").astype(jnp.int32)
    table = members.reshape(top, rows).T
    table = table[jax.random.permutation(jax.random.fold_in(own, 1), rows)]
    offset_by = jax.random.randint(jax.random.fold_in(own, 2), (rows, 1), 0, top)
    return jnp.take_along_axis(table, (jnp.arange(top)[None, :] + offset_by) % top, axis=1)


def shares(amount, total, bound, lean, full):
    portions = [(1 << 20) // math.isqrt(grade ** lean) + 1 for grade in range(1, amount + 1)]
    largest = bound if full else min(bound, max(-(-total // amount), total * portions[0] // sum(portions)))
    least = 1 if total - largest >= amount - 1 else 0
    given, surplus = [largest] + [least] * (amount - 1), total - largest - least * (amount - 1)
    while surplus > 0:
        candidates = [i for i in range(1, amount) if given[i] < largest] or [i for i in range(1, amount) if given[i] < bound]
        mass, budget = sum([portions[i] for i in candidates]), surplus
        for i in candidates:
            more = min(bound - given[i], max(1, budget * portions[i] // mass), surplus)
            given[i] = given[i] + more
            surplus = surplus - more
    return np.array(given)


def bell_draw(own_key, extent, width, bound, split=(), kind=jnp.bfloat16):
    loudness = steps_of(own_key, extent, split, -0.22, 0.18) if split else 1.0
    array = jax.random.normal(own_key, extent, jnp.float32) * width * loudness
    return jnp.minimum(jnp.maximum(array, -bound), bound).astype(kind)


def setup_inputs(seed: int = 0) -> dict:
    key_list = jax.random.split(jax.random.key(seed), 9)
    activations = bell_draw(key_list[0], (MICRO, TOKENS, D), 1.0, 6.0, ((1, 32),))
    norm_gain = jnp.clip(1.0 + 0.18 * jax.random.normal(key_list[1], (LAYERS, D), jnp.float32), 0.099609375, 1.8984375).astype(jnp.bfloat16)
    placement = jax.vmap(lambda own: jax.random.permutation(own, EXPERTS))(jax.random.split(key_list[2], LAYERS)).reshape((LAYERS, EXPERTS)).astype(jnp.int32)
    expert_ids_keys = jax.random.split(jax.random.fold_in(key_list[3], 1), LAYERS * MICRO * TOKENS // HB)
    expert_ids_turns = jax.random.permutation(jax.random.fold_in(key_list[3], 3), LAYERS * MICRO * TOKENS // HB)
    expert_ids = jax.vmap(lambda own, number: assign_block(jax.random.fold_in(key_list[3], 2), own, number, HB, EXPERTS, TOPK, MOSTH, 2))(expert_ids_keys, expert_ids_turns).reshape((LAYERS, MICRO, TOKENS, TOPK))
    expert_weights = jnp.clip(0.05 + 0.39999999 * jax.random.uniform(key_list[4], (LAYERS, MICRO, TOKENS, TOPK), jnp.float32) ** steps_of(key_list[4], (LAYERS, MICRO, TOKENS, TOPK), ((0, 8), (2, 32)), -0.2, 0.2), 0.05, 0.45)
    gate_store = bell_draw(key_list[5], (LAYERS, EXPERTS, D, FF), D ** -0.5, 0.125, ((0, 8), (1, 32)))
    up_store = bell_draw(key_list[6], (LAYERS, EXPERTS, D, FF), D ** -0.5, 0.125, ((0, 8), (1, 32)))
    down_store = bell_draw(key_list[7], (LAYERS, EXPERTS, FF, D), FF ** -0.5, 0.21875, ((0, 8), (1, 32)))
    return {"activations": activations, "norm_gain": norm_gain, "placement": placement, "expert_ids": expert_ids, "expert_weights": expert_weights, "gate_store": gate_store, "up_store": up_store, "down_store": down_store}


epsilon = 1e-06
tile_rows = 128

def norm_rows(values, gain):
    inverse = lax.rsqrt(lax.optimization_barrier(jnp.mean(values * values, axis=-1, keepdims=True)) + epsilon)
    return (values * inverse * gain).astype(jnp.bfloat16)

def expert_layer(layer_in, gain, route_rows, weight_rows, gate_w, up_w, down_w):
    token_total = layer_in.shape[0]
    top_count = route_rows.shape[1]
    expert_count = gate_w.shape[0]
    values = layer_in.astype(jnp.float32)
    normed = norm_rows(values, gain.astype(jnp.float32))
    flat_ids = route_rows.reshape(-1).astype(jnp.int32)
    pair_total = flat_ids.shape[0]
    onehot = (flat_ids[:, None] == jnp.arange(expert_count, dtype=jnp.int32)[None, :]).astype(jnp.int32)
    counts = lax.optimization_barrier(jnp.sum(onehot, axis=0))
    slot_rank = lax.optimization_barrier(jnp.sum((jnp.cumsum(onehot, axis=0) - onehot) * onehot, axis=1))
    padded = (counts + tile_rows - 1) // tile_rows * tile_rows
    seg_ends = jnp.cumsum(padded)
    seg_starts = seg_ends - padded
    position = (lax.optimization_barrier(jnp.sum(onehot * seg_starts[None, :], axis=1)) + slot_rank).astype(jnp.int32)
    tile_count = (pair_total + tile_rows - 1) // tile_rows + expert_count
    stream = tile_count * tile_rows
    token_of = jnp.arange(pair_total, dtype=jnp.int32) // top_count
    source = jnp.zeros((stream,), jnp.int32).at[position].set(token_of)
    filled = jnp.zeros((stream,), jnp.bool_).at[position].set(True)
    stream_rows = jnp.where(filled[:, None], normed[source], jnp.zeros((), jnp.bfloat16))
    tile_start = jnp.arange(tile_count, dtype=jnp.int32) * tile_rows
    tile_expert = jnp.minimum(lax.optimization_barrier(jnp.sum((seg_ends[None, :] <= tile_start[:, None]).astype(jnp.int32), axis=1)), expert_count - 1).astype(jnp.int32)

    def tile_apply(operands):
        block, which = operands
        block_wide = block.astype(jnp.float32)
        gate_value = jnp.dot(block_wide, gate_w[which], preferred_element_type=jnp.float32, precision=lax.Precision.HIGHEST)
        up_value = jnp.dot(block_wide, up_w[which], preferred_element_type=jnp.float32, precision=lax.Precision.HIGHEST)
        hidden = (jax.nn.silu(gate_value) * up_value).astype(jnp.bfloat16)
        return jnp.dot(hidden.astype(jnp.float32), down_w[which], preferred_element_type=jnp.float32, precision=lax.Precision.HIGHEST).astype(jnp.bfloat16)
    results = lax.map(tile_apply, (stream_rows.reshape(tile_count, tile_rows, -1), tile_expert))
    picked = results.reshape(stream, -1)[position].reshape(token_total, top_count, -1)
    mixed = lax.optimization_barrier(jnp.sum(weight_rows.astype(jnp.float32)[:, :, None] * picked.astype(jnp.float32), axis=1))
    return (values + mixed).astype(jnp.bfloat16)

def reference(activations, norm_gain, placement, expert_ids, expert_weights, gate_store, up_store, down_store):
    layer_list = []
    previous = [activations[piece] for piece in range(MICRO)]
    for layer in range(LAYERS):
        owner = jnp.argsort(placement[layer]).astype(jnp.int32)
        gate_w = gate_store[layer][owner].astype(jnp.float32)
        up_w = up_store[layer][owner].astype(jnp.float32)
        down_w = down_store[layer][owner].astype(jnp.float32)
        current = []
        for piece in range(MICRO):
            produced = expert_layer(previous[piece], norm_gain[layer], expert_ids[layer, piece], expert_weights[layer, piece], gate_w, up_w, down_w)
            current.append(produced)
        layer_list.append(jnp.stack(current))
        previous = current
    return jnp.stack(layer_list)
```

```python
import functools

import jax
import jax.numpy as jnp
from jax import lax
from jax.experimental import pallas as pl
from jax.experimental.pallas import tpu as pltpu
from jax.sharding import PartitionSpec as P

MESH = pl.DeviceIdType.MESH
epsilon = 1e-06
SIDE = 4
ROWS = 16


def layer_kernel(
    planes, pieces,
    act, gain, weight_table, gate_hbm, up_hbm, down_hbm,
    out,
    wg, wu, wd, xg, xn, hidden, rs1, rs2, rs3, part_o, part_m, fbuf, obuf,
    w_sem, x_recv, y_send, y_recv, s_send, s_recv, d_send, r1_recv, e_send, r2_recv, f_send, r3_recv,
    g_send, o_send, o_recv, i_send,
):
    half = xg.shape[-1]
    ff = wg.shape[-1]
    total = SIDE * SIDE * ROWS
    z = lax.axis_index("pipe")
    e = lax.axis_index("expert")
    core = e % 2
    chip = e // 2
    x, y = chip % SIDE, chip // SIDE
    other = 1 - core
    u = x * other + y * core
    v = y * other + x * core
    su, sv = 2 + (2 * SIDE - 2) * core, 2 * SIDE - (2 * SIDE - 2) * core

    def dev(u_at, v_at):
        return u_at * su + v_at * sv + core

    sibling = u * su + v * sv + other

    def cross(u_at, v_at):
        return u_at * su + v_at * sv + other

    def wait(sem, ref):
        pltpu.make_async_copy(ref, ref, sem).wait()

    def send(src, dst, send_sem, recv_sem, plane, device):
        pltpu.make_async_remote_copy(
            src_ref=src, dst_ref=dst, send_sem=send_sem, recv_sem=recv_sem,
            device_id=(plane, device), device_id_type=MESH,
        ).start()

    loads = []
    own = pl.ds(pl.multiple_of(core * half, 128), half)
    oth = pl.ds(pl.multiple_of(other * half, 128), half)
    for at, part in ((0, own), (1, oth)):
        rows = pl.ds(at * half, half)
        loads.append(pltpu.make_async_copy(gate_hbm.at[0, 0, part], wg.at[rows], w_sem.at[at]))
        loads.append(pltpu.make_async_copy(up_hbm.at[0, 0, part], wu.at[rows], w_sem.at[2 + at]))
        loads.append(
            pltpu.make_async_copy(down_hbm.at[0, 0, :, part], wd.at[at], w_sem.at[4 + at])
        )
    for load in loads:
        load.start()

    barrier = pltpu.get_barrier_semaphore()

    def greet(plane, device):
        pl.semaphore_signal(barrier, inc=1, device_id=(plane, device), device_id_type=MESH)

    greet(z, sibling)
    for k in range(1, SIDE):
        greet(z, dev(lax.rem(u + k, SIDE), v))
        greet(z, dev(u, lax.rem(v + k, SIDE)))

    @pl.when(z > 0)
    def _():
        for k in range(SIDE):
            greet(z - 1, dev(k, v))

    @pl.when(z == 0)
    def _():
        for k in range(1, SIDE):
            greet(z, cross(lax.rem(u + k, SIDE), v))

    first, last = jnp.where(z == 0, 1, 0), jnp.where(z == planes - 1, 1, 0)
    pl.semaphore_wait(barrier, 2 * SIDE - 1 + (SIDE - 1) * first + SIDE * (1 - last))

    def inject(p):
        q = p // 2

        @pl.when((z == 0) & (p < pieces) & (p % 2 == core))
        def _():
            pltpu.make_async_copy(act.at[core, q], xg.at[p, 0, v, u], x_recv.at[p]).start()
            for k in range(1, SIDE):
                send(act.at[core, q], xg.at[p, 0, v, u], i_send.at[p, 0], x_recv.at[p],
                     z, dev(lax.rem(u + k, SIDE), v))
            for k in range(SIDE):
                send(act.at[other, q], xg.at[p, 0, u, v], i_send.at[p, 1], x_recv.at[p],
                     z, cross(u, lax.rem(v + k, SIDE)))

    def relay(p, at):
        send(xg.at[p, 0, at], xg.at[p, 1, :, at], s_send.at[p], s_recv.at[p], z, sibling)

    def stage_a(p):
        wait(x_recv.at[p], xg.at[p, 0, v])
        for k in (2, 1, 3):
            send(xg.at[p, 0, v], xg.at[p, 0, v], y_send.at[p, k - 1], y_recv.at[p, k - 1],
                 z, dev(u, lax.rem(v + k, SIDE)))
        relay(p, v)

    def stage_b(p):
        for k in (1, 3, 2):
            at = lax.rem(v + SIDE - k, SIDE)
            wait(y_recv.at[p, k - 1], xg.at[p, 0, at])
            relay(p, at)

    def stage_norm(p):
        wait(s_recv.at[p], xg.at[p, 1])

        def block(r, _):
            for c in range(SIDE):
                x0 = xg[p, 0, r, c].astype(jnp.float32)
                x1 = xg[p, 1, r, c].astype(jnp.float32)
                square = jnp.sum(x0 * x0, axis=-1, keepdims=True)
                square = square + jnp.sum(x1 * x1, axis=-1, keepdims=True)
                inverse = lax.rsqrt(square / (2 * half) + epsilon)
                xn[r, c, :, 0:half] = (x0 * inverse * gain[0]).astype(jnp.bfloat16)
                xn[r, c, :, half:] = (x1 * inverse * gain[1]).astype(jnp.bfloat16)
            return 0

        lax.fori_loop(0, SIDE, block, 0)

    def stage_up(p):
        lane = lax.broadcasted_iota(jnp.int32, weight_table.shape, 1)
        scale = jnp.sum(jnp.where(lane == p, weight_table[...], 0.0), axis=1, keepdims=True)
        step = min(256, ff)
        rows = xn[...].reshape(total, 2 * half)
        for n in range(0, ff, step):
            gate_value = jnp.dot(rows, wg[:, n : n + step], preferred_element_type=jnp.float32)
            up_value = jnp.dot(rows, wu[:, n : n + step], preferred_element_type=jnp.float32)
            value = gate_value / (1.0 + jnp.exp(-gate_value)) * up_value * scale
            hidden[:, n : n + step] = value.astype(jnp.bfloat16)

    def stage_down(p):
        slot = p % 2

        @pl.when(p >= 2)
        def _():
            wait(d_send.at[p - 2], part_o.at[slot])
            wait(e_send.at[p - 2], part_m.at[slot, 0 : SIDE - 1])

        step = min(256, half)
        for at, part in ((1, part_o), (0, part_m)):
            for n in range(0, half, step):
                value = jnp.dot(
                    hidden[...], wd[at, :, n : n + step], preferred_element_type=jnp.float32
                )
                part[slot, :, :, :, n : n + step] = value.astype(jnp.bfloat16).reshape(
                    SIDE, SIDE, ROWS, step
                )
            if at == 1:
                for k in range(SIDE):
                    send(part_o.at[slot, k], rs1.at[slot, :, k], d_send.at[p], r1_recv.at[p],
                         z, sibling)

    def stage_e(p):
        slot = p % 2
        wait(r1_recv.at[p], rs1.at[slot])
        for k in (2, 1, 3, 0):
            at = lax.rem(v + k, SIDE)
            value = part_m[slot, at].astype(jnp.float32) + rs1[slot, at].astype(jnp.float32)
            part_m[slot, at] = value.astype(jnp.bfloat16)
            if k:
                send(part_m.at[slot, at], rs2.at[slot, k - 1], e_send.at[p], r2_recv.at[p],
                     z, dev(u, at))

    def stage_f(p):
        slot = p % 2
        wait(r2_recv.at[p], rs2.at[slot])

        @pl.when(p >= 2)
        def _():
            wait(f_send.at[p - 2], fbuf.at[slot, 0 : SIDE - 1])

        for k in (2, 1, 3, 0):
            at = lax.rem(u + k, SIDE)
            value = part_m[slot, v, at].astype(jnp.float32)
            for j in range(SIDE - 1):
                value = value + rs2[slot, j, at].astype(jnp.float32)
            fbuf[slot, at] = value.astype(jnp.bfloat16)
            if k:
                send(fbuf.at[slot, at], rs3.at[p, k - 1], f_send.at[p], r3_recv.at[p],
                     z, dev(at, v))

    def stage_g(p):
        slot = p % 2
        q = p // 2
        wait(r3_recv.at[p], rs3.at[p])
        value = xg[p, 0, v, u].astype(jnp.float32) + fbuf[slot, u].astype(jnp.float32)
        for j in range(SIDE - 1):
            value = value + rs3[p, j].astype(jnp.float32)
        obuf[p] = value.astype(jnp.bfloat16)

        @pl.when(z < planes - 1)
        def _():
            for k in range(SIDE):
                send(obuf.at[p], xg.at[p, 0, v, u], g_send.at[p], x_recv.at[p],
                     z + 1, dev(lax.rem(u + k, SIDE), v))

        @pl.when(p % 2 == core)
        def _():
            pltpu.make_async_copy(obuf.at[p], out.at[core, q], o_send.at[p]).start()

        @pl.when(p % 2 == other)
        def _():
            send(obuf.at[p], out.at[core, q], o_send.at[p], o_recv.at[p], z, sibling)

    inject(0)
    inject(1)

    def iteration(i, _):
        @pl.when(i < pieces)
        def _():
            stage_a(i)
            inject(i + 2)

        @pl.when(i >= 1)
        def _():
            stage_e(i - 1)

        @pl.when(i == 0)
        def _():
            for load in loads:
                load.wait()

        @pl.when(i < pieces)
        def _():
            stage_b(i)
            stage_norm(i)
            stage_up(i)

        @pl.when(i >= 1)
        def _():
            stage_f(i - 1)

        @pl.when(i < pieces)
        def _():
            stage_down(i)

        @pl.when(i >= 1)
        def _():
            stage_g(i - 1)

        return 0

    lax.fori_loop(0, pieces + 1, iteration, 0)

    def drain(p, _):
        for k in range(1, SIDE):
            wait(y_send.at[p, k - 1], xg.at[p, 0, v])
        wait(s_send.at[p], xg.at[p, 0])

        @pl.when(p >= pieces - 2)
        def _():
            wait(d_send.at[p], part_o.at[0])
            wait(e_send.at[p], part_m.at[0, 0 : SIDE - 1])
            wait(f_send.at[p], fbuf.at[0, 0 : SIDE - 1])

        @pl.when(z < planes - 1)
        def _():
            wait(g_send.at[p], xg.at[p, 0, v])

        wait(o_send.at[p], obuf.at[p])

        @pl.when(p % 2 == core)
        def _():
            wait(o_recv.at[p], obuf.at[p])

        @pl.when((z == 0) & (p % 2 == core))
        def _():
            wait(i_send.at[p, 0], xg.at[p, 0, v, 0 : SIDE - 1])
            wait(i_send.at[p, 1], xg.at[p, 0, v])

        return 0

    lax.fori_loop(0, pieces, drain, 0)


def on_device(
    activations, norm_gain, placement, expert_ids, expert_weights, gate_store, up_store, down_store
):
    planes = lax.axis_size("pipe")
    group = lax.axis_size("expert")
    core = lax.axis_index("expert") % 2
    micro, rows_local, width = activations.shape
    half = width // 2
    ff = gate_store.shape[-1]
    rows = micro * rows_local
    depth = rows // ROWS
    pieces = 2 * depth
    total = SIDE * SIDE * ROWS
    bf16 = jnp.bfloat16

    ids = expert_ids.reshape(1, rows, -1)
    weights = expert_weights.reshape(1, rows, -1)
    named = jnp.where(ids == placement[0][:, None, None], weights, 0.0)
    dense = jnp.sum(named, axis=-1)
    mine = lax.all_to_all(dense, "expert", split_axis=0, concat_axis=0, tiled=True)
    mine = mine.reshape(SIDE, SIDE, 2, depth, ROWS)
    table = jnp.where(
        core == 0, mine.transpose(0, 1, 4, 3, 2), mine.transpose(1, 0, 4, 3, 2)
    ).reshape(total, pieces)

    act = activations.reshape(depth, ROWS, 2, half).transpose(2, 0, 1, 3)
    gain = norm_gain[0].astype(jnp.float32).reshape(2, 1, half)
    gain = jnp.where(core == 0, gain, gain[::-1])

    dma = pltpu.SemaphoreType.DMA
    vmem = pl.BlockSpec(memory_space=pltpu.VMEM)
    hbm = pl.BlockSpec(memory_space=pl.ANY)
    out = pl.pallas_call(
        functools.partial(layer_kernel, planes, pieces),
        out_shape=jax.ShapeDtypeStruct((2, depth, ROWS, half), bf16),
        in_specs=[vmem, vmem, vmem, hbm, hbm, hbm],
        out_specs=vmem,
        scratch_shapes=[
            pltpu.VMEM((width, ff), bf16),
            pltpu.VMEM((width, ff), bf16),
            pltpu.VMEM((2, ff, half), bf16),
            pltpu.VMEM((pieces, 2, SIDE, SIDE, ROWS, half), bf16),
            pltpu.VMEM((SIDE, SIDE, ROWS, width), bf16),
            pltpu.VMEM((total, ff), bf16),
            pltpu.VMEM((2, SIDE, SIDE, ROWS, half), bf16),
            pltpu.VMEM((2, SIDE - 1, SIDE, ROWS, half), bf16),
            pltpu.VMEM((pieces, SIDE - 1, ROWS, half), bf16),
            pltpu.VMEM((2, SIDE, SIDE, ROWS, half), bf16),
            pltpu.VMEM((2, SIDE, SIDE, ROWS, half), bf16),
            pltpu.VMEM((2, SIDE, ROWS, half), bf16),
            pltpu.VMEM((pieces, ROWS, half), bf16),
            dma((6,)),
            dma((pieces,)),
            dma((pieces, SIDE - 1)),
            dma((pieces, SIDE - 1)),
            dma((pieces,)),
            dma((pieces,)),
            dma((pieces,)),
            dma((pieces,)),
            dma((pieces,)),
            dma((pieces,)),
            dma((pieces,)),
            dma((pieces,)),
            dma((pieces,)),
            dma((pieces,)),
            dma((pieces,)),
            dma((pieces, 2)),
        ],
        compiler_params=pltpu.CompilerParams(
            collective_id=0, has_side_effects=True, vmem_limit_bytes=60 * 2**20
        ),
        name="layers",
    )(act, gain, table, gate_store, up_store, down_store)
    return out.transpose(1, 2, 0, 3).reshape(1, micro, rows_local, width)


def solution(mesh):
    in_specs = (
        P(None, "expert", None),
        P("pipe", None),
        P("pipe", None),
        P("pipe", None, "expert", None),
        P("pipe", None, "expert", None),
        P("pipe", "expert", None, None),
        P("pipe", "expert", None, None),
        P("pipe", "expert", None, None),
    )
    out_specs = P("pipe", None, "expert", None)
    return jax.shard_map(
        on_device, mesh=mesh, in_specs=in_specs, out_specs=out_specs, check_vma=False
    )
```

```python
import functools

import jax
import jax.numpy as jnp
from jax import lax
from jax.experimental import pallas as pl
from jax.experimental.pallas import tpu as pltpu
from jax.sharding import PartitionSpec as P

MESH = pl.DeviceIdType.MESH
epsilon = 1e-06
SIDE = 4
ROWS = 16
DEPTH = 4
ORDER = (("a", 0), ("b", 1), ("e", 2), ("g", 4), ("f", 3), ("nud", 1))
LOADED = 1


def layer_kernel(
    planes, pieces,
    act, gain, weight_table, gate_hbm, up_hbm, down_hbm,
    out,
    wg, wu, wd, xg, xn, hidden, rs1, rs2, rs3, part_o, part_m, fbuf, obuf,
    w_sem, i_send, i_recv, h_send, x_recv, y_send, y_recv, s_send, s_recv, d_send, r1_recv, e_send, r2_recv,
    f_send, r3_recv, g_send, o_send, o_recv,
):
    block = xg.shape[-1]
    half = 2 * block
    ff = wg.shape[-1]
    groups = SIDE * SIDE // 2
    z = lax.axis_index("pipe")
    e = lax.axis_index("expert")
    core = e % 2
    chip = e // 2
    x, y = chip % SIDE, chip // SIDE
    other = 1 - core
    u = x * other + y * core
    v = y * other + x * core
    su, sv = 2 + (2 * SIDE - 2) * core, 2 * SIDE - (2 * SIDE - 2) * core
    parity = x % 2
    mine = 2 * parity + core

    def dev(u_at, v_at):
        return u_at * su + v_at * sv + core

    sibling = u * su + v * sv + other

    def member(number):
        return (y * SIDE + x - parity + number // 2) * 2 + number % 2

    def wait(sem, ref):
        pltpu.make_async_copy(ref, ref, sem).wait()

    def send(src, dst, send_sem, recv_sem, plane, device):
        pltpu.make_async_remote_copy(
            src_ref=src, dst_ref=dst, send_sem=send_sem, recv_sem=recv_sem,
            device_id=(plane, device), device_id_type=MESH,
        ).start()

    loads = []
    own = pl.ds(pl.multiple_of(core * half, 128), half)
    oth = pl.ds(pl.multiple_of(other * half, 128), half)
    for at, part in ((0, own), (1, oth)):
        rows = pl.ds(at * half, half)
        loads.append(pltpu.make_async_copy(gate_hbm.at[0, 0, part], wg.at[rows], w_sem.at[at]))
        loads.append(pltpu.make_async_copy(up_hbm.at[0, 0, part], wu.at[rows], w_sem.at[2 + at]))
        loads.append(
            pltpu.make_async_copy(down_hbm.at[0, 0, :, part], wd.at[at], w_sem.at[4 + at])
        )
    for load in loads:
        load.start()

    barrier = pltpu.get_barrier_semaphore()

    def greet(plane, device):
        pl.semaphore_signal(barrier, inc=1, device_id=(plane, device), device_id_type=MESH)

    greet(z, sibling)
    greet(z, member(3 - mine))
    for k in range(1, SIDE):
        greet(z, dev(lax.rem(u + k, SIDE), v))
        greet(z, dev(u, lax.rem(v + k, SIDE)))

    @pl.when(z > 0)
    def _():
        for k in range(SIDE):
            greet(z - 1, dev(k, v))

    last = jnp.where(z == planes - 1, 1, 0)
    pl.semaphore_wait(barrier, 2 * SIDE + SIDE * (1 - last))

    def inject(q):
        @pl.when((z == 0) & (4 * q < pieces))
        def _():
            p = 4 * q + mine
            pltpu.make_async_copy(act.at[mine, q], xg.at[p, 0, v, u], i_recv.at[p]).start()
            for k in range(1, 4):
                number = lax.rem(mine + k, 4)
                chip_at = x - parity + number // 2
                core_at = number % 2
                u_at = chip_at * (1 - core_at) + y * core_at
                v_at = y * (1 - core_at) + chip_at * core_at
                send(act.at[number, q], xg.at[p, 0, v_at, u_at], i_send.at[q], i_recv.at[p],
                     z, member(number))

    def stage_h(p):
        @pl.when(z == 0)
        def _():
            wait(i_recv.at[p], obuf.at[p])
            for k in (2, 1, 3):
                send(xg.at[p, 0, v, u], xg.at[p, 0, v, u], h_send.at[p], x_recv.at[p],
                     z, dev(lax.rem(u + k, SIDE), v))

    def relay(p, at):
        send(xg.at[p, 0, at], xg.at[p, 1, :, at], s_send.at[p], s_recv.at[p], z, sibling)

    def stage_a(p):
        @pl.when(z == 0)
        def _():
            wait(x_recv.at[p], xg.at[p, 0, v, 0 : SIDE - 1])

        @pl.when(z > 0)
        def _():
            wait(x_recv.at[p], xg.at[p, 0, v])

        for k in (2, 1, 3):
            send(xg.at[p, 0, v], xg.at[p, 0, v], y_send.at[p], y_recv.at[p, k - 1],
                 z, dev(u, lax.rem(v + k, SIDE)))
        relay(p, v)

    def stage_b(p):
        for k in (1, 3, 2):
            at = lax.rem(v + SIDE - k, SIDE)
            wait(y_recv.at[p, k - 1], xg.at[p, 0, at])
            relay(p, at)

    def place(y_at, x_at):
        return y_at * other + x_at * core, x_at * other + y_at * core

    def stage_n(p):
        wait(s_recv.at[p], xg.at[p, 1])

        def row(y_at, _):
            for j in range(SIDE // 2):
                quarters = []
                for at in range(2):
                    for par in range(2):
                        v_at, u_at = place(y_at, 2 * j + par)
                        quarters.append(xg[p, at, v_at, u_at].astype(jnp.float32))
                square = sum(jnp.sum(t * t, axis=-1, keepdims=True) for t in quarters)
                inverse = lax.rsqrt(square / (2 * half) + epsilon)
                for at, t in enumerate(quarters):
                    cut = slice(at * block, (at + 1) * block)
                    xn[y_at, j, :, cut] = (t * inverse * gain[:, cut]).astype(jnp.bfloat16)
            return 0

        lax.fori_loop(0, SIDE, row, 0)

    def stage_u(p):
        lane = lax.broadcasted_iota(jnp.int32, weight_table.shape, 1)
        scale = jnp.sum(jnp.where(lane == p, weight_table[...], 0.0), axis=1, keepdims=True)
        step = min(256, ff)
        rows = xn[...].reshape(groups * ROWS, 2 * half)
        for n in range(0, ff, step):
            gate_value = jnp.dot(rows, wg[:, n : n + step], preferred_element_type=jnp.float32)
            up_value = jnp.dot(rows, wu[:, n : n + step], preferred_element_type=jnp.float32)
            value = gate_value / (1.0 + jnp.exp(-gate_value)) * up_value * scale
            hidden[:, n : n + step] = value.astype(jnp.bfloat16)

    def stage_d(p):
        slot = p % DEPTH

        @pl.when(p >= DEPTH)
        def _():
            wait(d_send.at[p - DEPTH], part_o.at[slot])
            wait(e_send.at[p - DEPTH], part_m.at[slot, 0 : SIDE - 1])

        for at, part in ((1, part_o), (0, part_m)):
            value = jnp.dot(hidden[...], wd[at], preferred_element_type=jnp.float32)
            value = value.astype(jnp.bfloat16)
            for y_at in range(SIDE):
                for x_at in range(SIDE):
                    v_at, u_at = place(y_at, x_at)
                    top = (y_at * (SIDE // 2) + x_at // 2) * ROWS
                    left = x_at % 2 * block
                    part[slot, v_at, u_at] = value[top : top + ROWS, left : left + block]
            if at == 1:
                for k in range(SIDE):
                    send(part_o.at[slot, k], rs1.at[slot, :, k], d_send.at[p], r1_recv.at[p],
                         z, sibling)

    def stage_e(p):
        slot = p % DEPTH
        wait(r1_recv.at[p], rs1.at[slot])
        for k in (2, 1, 3, 0):
            at = lax.rem(v + k, SIDE)
            value = part_m[slot, at].astype(jnp.float32) + rs1[slot, at].astype(jnp.float32)
            part_m[slot, at] = value.astype(jnp.bfloat16)
            if k:
                send(part_m.at[slot, at], rs2.at[slot, k - 1], e_send.at[p], r2_recv.at[p],
                     z, dev(u, at))

    def stage_f(p):
        slot = p % DEPTH
        wait(r2_recv.at[p], rs2.at[slot])

        @pl.when(p >= DEPTH)
        def _():
            wait(f_send.at[p - DEPTH], fbuf.at[slot, 0 : SIDE - 1])

        for k in (2, 1, 3, 0):
            at = lax.rem(u + k, SIDE)
            value = part_m[slot, v, at].astype(jnp.float32)
            for j in range(SIDE - 1):
                value = value + rs2[slot, j, at].astype(jnp.float32)
            fbuf[slot, at] = value.astype(jnp.bfloat16)
            if k:
                send(fbuf.at[slot, at], rs3.at[p, k - 1], f_send.at[p], r3_recv.at[p],
                     z, dev(at, v))

    def stage_g(p):
        slot = p % DEPTH
        q = p // 4
        wait(r3_recv.at[p], rs3.at[p])
        value = xg[p, 0, v, u].astype(jnp.float32) + fbuf[slot, u].astype(jnp.float32)
        for j in range(SIDE - 1):
            value = value + rs3[p, j].astype(jnp.float32)
        obuf[p] = value.astype(jnp.bfloat16)

        @pl.when(z < planes - 1)
        def _():
            for k in (2, 1, 3, 0):
                send(obuf.at[p], xg.at[p, 0, v, u], g_send.at[p], x_recv.at[p],
                     z + 1, dev(lax.rem(u + k, SIDE), v))

        @pl.when(p % 4 == mine)
        def _():
            pltpu.make_async_copy(obuf.at[p], out.at[mine, q], o_send.at[p]).start()

        @pl.when(p % 4 != mine)
        def _():
            send(obuf.at[p], out.at[mine, q], o_send.at[p], o_recv.at[p], z, member(p % 4))

    inject(0)
    inject(1)
    stage_h(0)

    stages = dict(a=stage_a, b=stage_b, n=stage_n, u=stage_u, d=stage_d, e=stage_e, f=stage_f, g=stage_g)
    ahead = max(lag for _, lag in ORDER)

    def iteration(i, _):
        @pl.when(i == LOADED)
        def _():
            for load in loads:
                load.wait()

        @pl.when(i % 4 == 0)
        def _():
            inject(i // 4 + 2)

        @pl.when(i + 1 < pieces)
        def _():
            stage_h(i + 1)

        for names, lag in ORDER:

            @pl.when((i >= lag) & (i - lag < pieces))
            def _(names=names, lag=lag):
                for name in names:
                    stages[name](i - lag)

        return 0

    lax.fori_loop(0, pieces + ahead, iteration, 0)

    def drain(p, _):
        wait(y_send.at[p], xg.at[p, 0, 0 : SIDE - 1])
        wait(s_send.at[p], xg.at[p, 0])

        @pl.when(p >= pieces - DEPTH)
        def _():
            wait(d_send.at[p], part_o.at[0])
            wait(e_send.at[p], part_m.at[0, 0 : SIDE - 1])
            wait(f_send.at[p], fbuf.at[0, 0 : SIDE - 1])

        @pl.when(z < planes - 1)
        def _():
            wait(g_send.at[p], xg.at[p, 0, v])

        wait(o_send.at[p], obuf.at[p])

        @pl.when(p % 4 == mine)
        def _():
            wait(o_recv.at[p], xg.at[p, 0, 0, 0 : SIDE - 1])

        @pl.when(z == 0)
        def _():
            wait(h_send.at[p], xg.at[p, 0, v, 0 : SIDE - 1])

        @pl.when((z == 0) & (p % 4 == mine))
        def _():
            wait(i_send.at[p // 4], xg.at[p, 0, 0, 0 : SIDE - 1])

        return 0

    lax.fori_loop(0, pieces, drain, 0)


def on_device(
    activations, norm_gain, placement, expert_ids, expert_weights, gate_store, up_store, down_store
):
    planes = lax.axis_size("pipe")
    core = lax.axis_index("expert") % 2
    micro, rows_local, width = activations.shape
    half, block = width // 2, width // 4
    ff = gate_store.shape[-1]
    rows = micro * rows_local
    depth = rows // ROWS
    pieces = 4 * depth
    total = SIDE * SIDE // 2 * ROWS
    bf16 = jnp.bfloat16

    ids = expert_ids.reshape(1, rows, -1)
    weights = expert_weights.reshape(1, rows, -1)
    named = jnp.where(ids == placement[0][:, None, None], weights, 0.0)
    dense = jnp.sum(named, axis=-1)
    table = lax.all_to_all(dense, "expert", split_axis=0, concat_axis=0, tiled=True)
    table = table.reshape(SIDE, SIDE // 2, 4, depth, ROWS).transpose(0, 1, 4, 3, 2)
    table = table.reshape(total, pieces)

    act = activations.reshape(depth, ROWS, 2, 2, block).transpose(3, 2, 0, 1, 4)
    act = act.reshape(4, depth, ROWS, block)
    gain = norm_gain[0].astype(jnp.float32).reshape(2, half)
    gain = jnp.where(core == 0, gain, gain[::-1]).reshape(1, width)

    dma = pltpu.SemaphoreType.DMA
    vmem = pl.BlockSpec(memory_space=pltpu.VMEM)
    hbm = pl.BlockSpec(memory_space=pl.ANY)
    out = pl.pallas_call(
        functools.partial(layer_kernel, planes, pieces),
        out_shape=jax.ShapeDtypeStruct((4, depth, ROWS, block), bf16),
        in_specs=[vmem, vmem, vmem, hbm, hbm, hbm],
        out_specs=vmem,
        scratch_shapes=[
            pltpu.VMEM((width, ff), bf16),
            pltpu.VMEM((width, ff), bf16),
            pltpu.VMEM((2, ff, half), bf16),
            pltpu.VMEM((pieces, 2, SIDE, SIDE, ROWS, block), bf16),
            pltpu.VMEM((SIDE, SIDE // 2, ROWS, width), bf16),
            pltpu.VMEM((total, ff), bf16),
            pltpu.VMEM((DEPTH, SIDE, SIDE, ROWS, block), bf16),
            pltpu.VMEM((DEPTH, SIDE - 1, SIDE, ROWS, block), bf16),
            pltpu.VMEM((pieces, SIDE - 1, ROWS, block), bf16),
            pltpu.VMEM((DEPTH, SIDE, SIDE, ROWS, block), bf16),
            pltpu.VMEM((DEPTH, SIDE, SIDE, ROWS, block), bf16),
            pltpu.VMEM((DEPTH, SIDE, ROWS, block), bf16),
            pltpu.VMEM((pieces, ROWS, block), bf16),
            dma((6,)),
            dma((depth,)),
            *[dma((pieces,))] * 4,
            dma((pieces, SIDE - 1)),
            *[dma((pieces,))] * 11,
        ],
        compiler_params=pltpu.CompilerParams(
            collective_id=0, has_side_effects=True, vmem_limit_bytes=60 * 2**20
        ),
        name="layers",
    )(act, gain, table, gate_store, up_store, down_store)
    out = out.reshape(2, 2, depth, ROWS, block).transpose(2, 3, 1, 0, 4)
    return out.reshape(1, micro, rows_local, width)


def solution(mesh):
    in_specs = (
        P(None, "expert", None),
        P("pipe", None),
        P("pipe", None),
        P("pipe", None, "expert", None),
        P("pipe", None, "expert", None),
        P("pipe", "expert", None, None),
        P("pipe", "expert", None, None),
        P("pipe", "expert", None, None),
    )
    out_specs = P("pipe", None, "expert", None)
    return jax.shard_map(
        on_device, mesh=mesh, in_specs=in_specs, out_specs=out_specs, check_vma=False
    )
```

```python
import functools

import jax
import jax.numpy as jnp
from jax import lax
from jax.experimental import pallas as pl
from jax.experimental.pallas import tpu as pltpu
from jax.sharding import PartitionSpec as P

MESH = pl.DeviceIdType.MESH
epsilon = 1e-06
SIDE = 4
ROWS = 16
DEPTH = 4
ORDER = (("a", 0), ("b", 1), ("e", 2), ("g", 4), ("f", 3), ("nud", 1))
LOADED = 1


def layer_kernel(
    planes, pieces,
    act, gain_row, ids, weights, slots, gate_hbm, up_hbm, down_hbm,
    out,
    gain, told, table, wg, wu, wd, xg, xn, hidden, rs1, rs2, rs3, part_o, part_m, fbuf, obuf,
    w_sem, t_send, t_recv, i_send, i_recv, h_send, x_recv, y_send, y_recv, s_send, s_recv, d_send, r1_recv, e_send, r2_recv,
    f_send, r3_recv, g_send, o_send, o_recv,
):
    block = xg.shape[-1]
    half = 2 * block
    ff = wg.shape[-1]
    groups = SIDE * SIDE // 2
    z = lax.axis_index("pipe")
    e = lax.axis_index("expert")
    core = e % 2
    chip = e // 2
    x, y = chip % SIDE, chip // SIDE
    other = 1 - core
    u = x * other + y * core
    v = y * other + x * core
    su, sv = 2 + (2 * SIDE - 2) * core, 2 * SIDE - (2 * SIDE - 2) * core
    parity = x % 2
    per_micro = act.shape[1] // ROWS
    mine = 2 * parity + core

    def dev(u_at, v_at):
        return u_at * su + v_at * sv + core

    sibling = u * su + v * sv + other

    def member(number):
        return (y * SIDE + x - parity + number // 2) * 2 + number % 2

    def wait(sem, ref):
        pltpu.make_async_copy(ref, ref, sem).wait()

    def send(src, dst, send_sem, recv_sem, plane, device):
        pltpu.make_async_remote_copy(
            src_ref=src, dst_ref=dst, send_sem=send_sem, recv_sem=recv_sem,
            device_id=(plane, device), device_id_type=MESH,
        ).start()

    loads = []
    own = pl.ds(pl.multiple_of(core * half, 128), half)
    oth = pl.ds(pl.multiple_of(other * half, 128), half)
    for at, part in ((0, own), (1, oth)):
        rows = pl.ds(at * half, half)
        loads.append(pltpu.make_async_copy(gate_hbm.at[0, 0, part], wg.at[rows], w_sem.at[at]))
        loads.append(pltpu.make_async_copy(up_hbm.at[0, 0, part], wu.at[rows], w_sem.at[2 + at]))
        loads.append(
            pltpu.make_async_copy(down_hbm.at[0, 0, :, part], wd.at[at], w_sem.at[4 + at])
        )
    for load in loads:
        load.start()

    barrier = pltpu.get_barrier_semaphore()

    def greet(plane, device):
        pl.semaphore_signal(barrier, inc=1, device_id=(plane, device), device_id_type=MESH)

    members = 2 * SIDE * SIDE

    def greet_all(k, _):
        greet(z, lax.rem(e + k, members))
        return 0

    lax.fori_loop(1, members, greet_all, 0)

    @pl.when(z > 0)
    def _():
        for k in range(SIDE):
            greet(z - 1, dev(k, v))

    last = jnp.where(z == planes - 1, 1, 0)

    for number in range(members):
        expert = slots[0, number]
        value = jnp.zeros((8, ids.shape[1]), jnp.float32)
        for k in range(ids.shape[0]):
            value = value + jnp.where(ids[k : k + 1, :] == expert, weights[k : k + 1, :], 0.0)
        told[number] = value
    gain[:, 0:half] = gain_row[:, own]
    gain[:, half:] = gain_row[:, oth]

    pl.semaphore_wait(barrier, members - 1 + SIDE * (1 - last))

    def tell():
        group = y * (SIDE // 2) + x // 2
        pltpu.make_async_copy(told.at[e], table.at[mine, group], t_recv).start()

        def one(k, _):
            device = lax.rem(e + k, members)
            send(told.at[device], table.at[mine, group], t_send, t_recv, z, device)
            return 0

        lax.fori_loop(1, members, one, 0)

    def rows_of(ref, q, number):
        left = pl.multiple_of((number % 2 * 2 + number // 2) * block, 128)
        top = pl.multiple_of(q % per_micro * ROWS, ROWS)
        return ref.at[q // per_micro, pl.ds(top, ROWS), pl.ds(left, block)]

    def inject(q):
        @pl.when((z == 0) & (4 * q < pieces))
        def _():
            p = 4 * q + mine
            pltpu.make_async_copy(rows_of(act, q, mine), xg.at[p, 0, v, u], i_recv.at[p]).start()
            for k in range(1, 4):
                number = lax.rem(mine + k, 4)
                chip_at = x - parity + number // 2
                core_at = number % 2
                u_at = chip_at * (1 - core_at) + y * core_at
                v_at = y * (1 - core_at) + chip_at * core_at
                send(rows_of(act, q, number), xg.at[p, 0, v_at, u_at], i_send.at[q], i_recv.at[p],
                     z, member(number))

    def stage_h(p):
        @pl.when(z == 0)
        def _():
            wait(i_recv.at[p], obuf.at[p])
            for k in (1, 3, 2):
                send(xg.at[p, 0, v, u], xg.at[p, 0, v, u], h_send.at[p], x_recv.at[p, k],
                     z, dev(lax.rem(u + k, SIDE), v))

    def relay(p, at):
        send(xg.at[p, 0, at], xg.at[p, 1, :, at], s_send.at[p], s_recv.at[p], z, sibling)

    def stage_a(p):
        for k in (0, 1, 3, 2):
            at = lax.rem(u + SIDE - k, SIDE)
            if k:
                wait(x_recv.at[p, k], obuf.at[p])
            else:

                @pl.when(z > 0)
                def _():
                    wait(x_recv.at[p, 0], obuf.at[p])

            for j in (2, 1, 3):
                send(xg.at[p, 0, v, at], xg.at[p, 0, v, at], y_send.at[p], y_recv.at[p, j - 1],
                     z, dev(u, lax.rem(v + j, SIDE)))
            send(xg.at[p, 0, v, at], xg.at[p, 1, at, v], s_send.at[p], s_recv.at[p], z, sibling)

    def stage_b(p):
        for k in (1, 3, 2):
            at = lax.rem(v + SIDE - k, SIDE)
            wait(y_recv.at[p, k - 1], xg.at[p, 0, at])
            relay(p, at)

    def place(y_at, x_at):
        return y_at * other + x_at * core, x_at * other + y_at * core

    def stage_n(p):
        wait(s_recv.at[p], xg.at[p, 1])

        def row(y_at, _):
            for j in range(SIDE // 2):
                quarters = []
                for at in range(2):
                    for par in range(2):
                        v_at, u_at = place(y_at, 2 * j + par)
                        quarters.append(xg[p, at, v_at, u_at].astype(jnp.float32))
                square = sum(jnp.sum(t * t, axis=-1, keepdims=True) for t in quarters)
                inverse = lax.rsqrt(square / (2 * half) + epsilon)
                for at, t in enumerate(quarters):
                    cut = slice(at * block, (at + 1) * block)
                    xn[y_at, j, :, cut] = (t * inverse * gain[:, cut]).astype(jnp.bfloat16)
            return 0

        lax.fori_loop(0, SIDE, row, 0)

    def stage_u(p):
        @pl.when(p == 0)
        def _():
            wait(t_recv, table)

        named = table[p % 4]
        named = jnp.concatenate([named, named], axis=1)
        token = p // 4 * ROWS + lax.broadcasted_iota(jnp.int32, named.shape, 1)
        lane = lax.broadcasted_iota(jnp.int32, named.shape, 2)
        scale = jnp.sum(jnp.where(lane == token, named, 0.0), axis=2, keepdims=True)
        scale = scale.reshape(groups * ROWS, 1)
        step = min(256, ff)
        rows = xn[...].reshape(groups * ROWS, 2 * half)
        for n in range(0, ff, step):
            gate_value = jnp.dot(rows, wg[:, n : n + step], preferred_element_type=jnp.float32)
            up_value = jnp.dot(rows, wu[:, n : n + step], preferred_element_type=jnp.float32)
            value = gate_value / (1.0 + jnp.exp(-gate_value)) * up_value * scale
            hidden[:, n : n + step] = value.astype(jnp.bfloat16)

    def stage_d(p):
        slot = p % DEPTH

        @pl.when(p >= DEPTH)
        def _():
            wait(d_send.at[p - DEPTH], part_o.at[slot])
            wait(e_send.at[p - DEPTH], part_m.at[slot, 0 : SIDE - 1])

        for at, part in ((1, part_o), (0, part_m)):
            value = jnp.dot(hidden[...], wd[at], preferred_element_type=jnp.float32)
            value = value.astype(jnp.bfloat16)
            for y_at in range(SIDE):
                for x_at in range(SIDE):
                    v_at, u_at = place(y_at, x_at)
                    top = (y_at * (SIDE // 2) + x_at // 2) * ROWS
                    left = x_at % 2 * block
                    part[slot, v_at, u_at] = value[top : top + ROWS, left : left + block]
            if at == 1:
                for k in range(SIDE):
                    send(part_o.at[slot, k], rs1.at[slot, :, k], d_send.at[p], r1_recv.at[p],
                         z, sibling)

    def stage_e(p):
        slot = p % DEPTH
        wait(r1_recv.at[p], rs1.at[slot])
        for k in (2, 1, 3, 0):
            at = lax.rem(v + k, SIDE)
            value = part_m[slot, at].astype(jnp.float32) + rs1[slot, at].astype(jnp.float32)
            part_m[slot, at] = value.astype(jnp.bfloat16)
            if k:
                send(part_m.at[slot, at], rs2.at[slot, k - 1], e_send.at[p], r2_recv.at[p],
                     z, dev(u, at))

    def stage_f(p):
        slot = p % DEPTH
        wait(r2_recv.at[p], rs2.at[slot])

        @pl.when(p >= DEPTH)
        def _():
            wait(f_send.at[p - DEPTH], fbuf.at[slot, 0 : SIDE - 1])

        for k in (2, 1, 3, 0):
            at = lax.rem(u + k, SIDE)
            value = part_m[slot, v, at].astype(jnp.float32)
            for j in range(SIDE - 1):
                value = value + rs2[slot, j, at].astype(jnp.float32)
            fbuf[slot, at] = value.astype(jnp.bfloat16)
            if k:
                send(fbuf.at[slot, at], rs3.at[p, k - 1], f_send.at[p], r3_recv.at[p],
                     z, dev(at, v))

    def stage_g(p):
        slot = p % DEPTH
        q = p // 4
        wait(r3_recv.at[p], rs3.at[p])
        value = xg[p, 0, v, u].astype(jnp.float32) + fbuf[slot, u].astype(jnp.float32)
        for j in range(SIDE - 1):
            value = value + rs3[p, j].astype(jnp.float32)
        obuf[p] = value.astype(jnp.bfloat16)

        @pl.when(z < planes - 1)
        def _():
            for k in (0, 1, 3, 2):
                send(obuf.at[p], xg.at[p, 0, v, u], g_send.at[p], x_recv.at[p, k],
                     z + 1, dev(lax.rem(u + k, SIDE), v))

        @pl.when(p % 4 == mine)
        def _():
            pltpu.make_async_copy(obuf.at[p], rows_of(out, q, mine), o_send.at[p]).start()

        @pl.when(p % 4 != mine)
        def _():
            send(obuf.at[p], rows_of(out, q, mine), o_send.at[p], o_recv.at[p], z, member(p % 4))

    inject(0)
    tell()
    inject(1)
    stage_h(0)

    stages = dict(a=stage_a, b=stage_b, n=stage_n, u=stage_u, d=stage_d, e=stage_e, f=stage_f, g=stage_g)
    ahead = max(lag for _, lag in ORDER)

    def iteration(i, _):
        @pl.when(i == LOADED)
        def _():
            for load in loads:
                load.wait()

        @pl.when(i % 4 == 0)
        def _():
            inject(i // 4 + 2)

        @pl.when(i + 1 < pieces)
        def _():
            stage_h(i + 1)

        for names, lag in ORDER:

            @pl.when((i >= lag) & (i - lag < pieces))
            def _(names=names, lag=lag):
                for name in names:
                    stages[name](i - lag)

        return 0

    lax.fori_loop(0, pieces + ahead, iteration, 0)

    def drain(p, _):
        wait(y_send.at[p], xg.at[p, 0, 0 : SIDE - 1])
        wait(s_send.at[p], xg.at[p, 0])

        @pl.when(p >= pieces - DEPTH)
        def _():
            wait(d_send.at[p], part_o.at[0])
            wait(e_send.at[p], part_m.at[0, 0 : SIDE - 1])
            wait(f_send.at[p], fbuf.at[0, 0 : SIDE - 1])

        @pl.when(z < planes - 1)
        def _():
            wait(g_send.at[p], xg.at[p, 0, v])

        wait(o_send.at[p], obuf.at[p])

        @pl.when(p % 4 == mine)
        def _():
            wait(o_recv.at[p], xg.at[p, 0, 0, 0 : SIDE - 1])

        @pl.when(z == 0)
        def _():
            wait(h_send.at[p], xg.at[p, 0, v, 0 : SIDE - 1])

        @pl.when((z == 0) & (p % 4 == mine))
        def _():
            wait(i_send.at[p // 4], xg.at[p, 0, 0, 0 : SIDE - 1])

        return 0

    lax.fori_loop(0, pieces, drain, 0)
    wait(t_send, told.at[0 : members - 1])


def on_device(
    activations, norm_gain, placement, expert_ids, expert_weights, gate_store, up_store, down_store
):
    planes = lax.axis_size("pipe")
    members = lax.axis_size("expert")
    micro, rows_local, width = activations.shape
    half, block = width // 2, width // 4
    ff = gate_store.shape[-1]
    rows = micro * rows_local
    depth = rows // ROWS
    pieces = 4 * depth
    total = SIDE * SIDE // 2 * ROWS
    bf16 = jnp.bfloat16
    ids = expert_ids.reshape(rows, -1).T
    weights = expert_weights.reshape(rows, -1).T

    dma = pltpu.SemaphoreType.DMA
    vmem = pl.BlockSpec(memory_space=pltpu.VMEM)
    smem = pl.BlockSpec(memory_space=pltpu.SMEM)
    hbm = pl.BlockSpec(memory_space=pl.ANY)
    out = pl.pallas_call(
        functools.partial(layer_kernel, planes, pieces),
        out_shape=jax.ShapeDtypeStruct((micro, rows_local, width), bf16),
        in_specs=[hbm, vmem, vmem, vmem, smem, hbm, hbm, hbm],
        out_specs=vmem,
        scratch_shapes=[
            pltpu.VMEM((1, width), jnp.float32),
            pltpu.VMEM((members, 8, rows), jnp.float32),
            pltpu.VMEM((4, SIDE * SIDE // 2, 8, rows), jnp.float32),
            pltpu.VMEM((width, ff), bf16),
            pltpu.VMEM((width, ff), bf16),
            pltpu.VMEM((2, ff, half), bf16),
            pltpu.VMEM((pieces, 2, SIDE, SIDE, ROWS, block), bf16),
            pltpu.VMEM((SIDE, SIDE // 2, ROWS, width), bf16),
            pltpu.VMEM((total, ff), bf16),
            pltpu.VMEM((DEPTH, SIDE, SIDE, ROWS, block), bf16),
            pltpu.VMEM((DEPTH, SIDE - 1, SIDE, ROWS, block), bf16),
            pltpu.VMEM((pieces, SIDE - 1, ROWS, block), bf16),
            pltpu.VMEM((DEPTH, SIDE, SIDE, ROWS, block), bf16),
            pltpu.VMEM((DEPTH, SIDE, SIDE, ROWS, block), bf16),
            pltpu.VMEM((DEPTH, SIDE, ROWS, block), bf16),
            pltpu.VMEM((pieces, ROWS, block), bf16),
            dma((6,)),
            dma,
            dma,
            dma((depth,)),
            dma((pieces,)),
            dma((pieces,)),
            dma((pieces, SIDE)),
            dma((pieces,)),
            dma((pieces, SIDE - 1)),
            *[dma((pieces,))] * 11,
        ],
        compiler_params=pltpu.CompilerParams(
            collective_id=0, has_side_effects=True, vmem_limit_bytes=60 * 2**20
        ),
        name="layers",
    )(activations, norm_gain.astype(jnp.float32), ids, weights, placement, gate_store, up_store, down_store)
    return out[None]


def solution(mesh):
    in_specs = (
        P(None, "expert", None),
        P("pipe", None),
        P("pipe", None),
        P("pipe", None, "expert", None),
        P("pipe", None, "expert", None),
        P("pipe", "expert", None, None),
        P("pipe", "expert", None, None),
        P("pipe", "expert", None, None),
    )
    out_specs = P("pipe", None, "expert", None)
    return jax.shard_map(
        on_device, mesh=mesh, in_specs=in_specs, out_specs=out_specs, check_vma=False
    )
```

```python
import functools

import jax
import jax.numpy as jnp
from jax import lax
from jax.experimental import pallas as pl
from jax.experimental.pallas import tpu as pltpu
from jax.sharding import PartitionSpec as P

MESH = pl.DeviceIdType.MESH
epsilon = 1e-06
SIDE = 4
ROWS = 16
DEPTH = 4
ORDER = (("a", 0), ("b", 1), ("e", 2), ("g", 4), ("f", 3), ("nud", 1))
LOADED = 1


def layer_kernel(
    planes, pieces,
    act, gain_row, ids, weights, slots, gate_hbm, up_hbm, down_hbm,
    out,
    gain, told, table, wg, wu, wd, xg, xn, hidden, rs1, rs2, rs3, part_o, part_m, fbuf, obuf,
    w_sem, t_send, t_recv, i_send, i_recv, h_send, x_recv, y_send, y_recv, s_send, s_recv, d_send, r1_recv, e_send, r2_recv,
    f_send, r3_recv, g_send, o_send, o_recv,
):
    block = xg.shape[-1]
    half = 2 * block
    ff = wg.shape[-1]
    groups = SIDE * SIDE // 2
    z = lax.axis_index("pipe")
    e = lax.axis_index("expert")
    core = e % 2
    chip = e // 2
    x, y = chip % SIDE, chip // SIDE
    other = 1 - core
    u = x * other + y * core
    v = y * other + x * core
    su, sv = 2 + (2 * SIDE - 2) * core, 2 * SIDE - (2 * SIDE - 2) * core
    parity = x % 2
    per_micro = act.shape[1] // ROWS
    mine = 2 * parity + core

    def dev(u_at, v_at):
        return u_at * su + v_at * sv + core

    sibling = u * su + v * sv + other

    def member(number):
        return (y * SIDE + x - parity + number // 2) * 2 + number % 2

    def wait(sem, ref):
        pltpu.make_async_copy(ref, ref, sem).wait()

    def send(src, dst, send_sem, recv_sem, plane, device):
        pltpu.make_async_remote_copy(
            src_ref=src, dst_ref=dst, send_sem=send_sem, recv_sem=recv_sem,
            device_id=(plane, device), device_id_type=MESH,
        ).start()

    loads = []
    own = pl.ds(pl.multiple_of(core * half, 128), half)
    oth = pl.ds(pl.multiple_of(other * half, 128), half)
    for at, part in ((0, own), (1, oth)):
        rows = pl.ds(at * half, half)
        loads.append(pltpu.make_async_copy(gate_hbm.at[0, 0, part], wg.at[rows], w_sem.at[at]))
        loads.append(pltpu.make_async_copy(up_hbm.at[0, 0, part], wu.at[rows], w_sem.at[2 + at]))
        loads.append(
            pltpu.make_async_copy(down_hbm.at[0, 0, :, part], wd.at[at], w_sem.at[4 + at])
        )
    for load in loads:
        load.start()

    barrier = pltpu.get_barrier_semaphore()

    def greet(plane, device):
        pl.semaphore_signal(barrier, inc=1, device_id=(plane, device), device_id_type=MESH)

    members = 2 * SIDE * SIDE

    def greet_all(k, _):
        greet(z, lax.rem(e + k, members))
        return 0

    lax.fori_loop(1, members, greet_all, 0)

    @pl.when(z > 0)
    def _():
        for k in range(SIDE):
            greet(z - 1, dev(k, v))

    last = jnp.where(z == planes - 1, 1, 0)

    for number in range(members):
        expert = slots[0, number]
        value = jnp.zeros((8, ids.shape[1]), jnp.float32)
        for k in range(ids.shape[0]):
            value = value + jnp.where(ids[k : k + 1, :] == expert, weights[k : k + 1, :], 0.0)
        told[number] = value
    gain[:, 0:half] = gain_row[:, own]
    gain[:, half:] = gain_row[:, oth]

    pl.semaphore_wait(barrier, members - 1 + SIDE * (1 - last))

    def tell():
        group = y * (SIDE // 2) + x // 2
        pltpu.make_async_copy(told.at[e], table.at[mine, group], t_recv).start()

        def one(k, _):
            device = lax.rem(e + k, members)
            send(told.at[device], table.at[mine, group], t_send, t_recv, z, device)
            return 0

        lax.fori_loop(1, members, one, 0)

    def rows_of(ref, q, number):
        left = pl.multiple_of((number % 2 * 2 + number // 2) * block, 128)
        top = pl.multiple_of(q % per_micro * ROWS, ROWS)
        return ref.at[q // per_micro, pl.ds(top, ROWS), pl.ds(left, block)]

    def inject(q):
        @pl.when((z == 0) & (4 * q < pieces))
        def _():
            p = 4 * q + mine
            pltpu.make_async_copy(rows_of(act, q, mine), xg.at[p, 0, v, u], i_recv.at[p]).start()
            for k in range(1, 4):
                number = lax.rem(mine + k, 4)
                chip_at = x - parity + number // 2
                core_at = number % 2
                u_at = chip_at * (1 - core_at) + y * core_at
                v_at = y * (1 - core_at) + chip_at * core_at
                send(rows_of(act, q, number), xg.at[p, 0, v_at, u_at], i_send.at[q], i_recv.at[p],
                     z, member(number))

    def stage_h(p):
        @pl.when(z == 0)
        def _():
            wait(i_recv.at[p], obuf.at[p])
            for k in (1, 3, 2):
                send(xg.at[p, 0, v, u], xg.at[p, 0, v, u], h_send.at[p], x_recv.at[p, k],
                     z, dev(lax.rem(u + k, SIDE), v))

    def relay(p, at):
        send(xg.at[p, 0, at], xg.at[p, 1, :, at], s_send.at[p], s_recv.at[p], z, sibling)

    def stage_a(p):
        for k in (0, 1, 3, 2):
            at = lax.rem(u + SIDE - k, SIDE)
            if k:
                wait(x_recv.at[p, k], obuf.at[p])
            else:

                @pl.when(z > 0)
                def _():
                    wait(x_recv.at[p, 0], obuf.at[p])

            for j in (2, 1, 3):
                send(xg.at[p, 0, v, at], xg.at[p, 0, v, at], y_send.at[p], y_recv.at[p, j - 1],
                     z, dev(u, lax.rem(v + j, SIDE)))
            send(xg.at[p, 0, v, at], xg.at[p, 1, at, v], s_send.at[p], s_recv.at[p], z, sibling)

    def stage_b(p):
        for k in (1, 3, 2):
            at = lax.rem(v + SIDE - k, SIDE)
            wait(y_recv.at[p, k - 1], xg.at[p, 0, at])
            relay(p, at)

    def place(y_at, x_at):
        return y_at * other + x_at * core, x_at * other + y_at * core

    def stage_n(p):
        wait(s_recv.at[p], xg.at[p, 1])

        def row(y_at, _):
            for j in range(SIDE // 2):
                quarters = []
                for at in range(2):
                    for par in range(2):
                        v_at, u_at = place(y_at, 2 * j + par)
                        quarters.append(xg[p, at, v_at, u_at].astype(jnp.float32))
                square = sum(jnp.sum(t * t, axis=-1, keepdims=True) for t in quarters)
                inverse = lax.rsqrt(square / (2 * half) + epsilon)
                for at, t in enumerate(quarters):
                    cut = slice(at * block, (at + 1) * block)
                    xn[y_at, j, :, cut] = (t * inverse * gain[:, cut]).astype(jnp.bfloat16)
            return 0

        lax.fori_loop(0, SIDE, row, 0)

    def stage_u(p):
        @pl.when(p == 0)
        def _():
            wait(t_recv, table)

        named = table[p % 4]
        named = jnp.concatenate([named, named], axis=1)
        token = p // 4 * ROWS + lax.broadcasted_iota(jnp.int32, named.shape, 1)
        lane = lax.broadcasted_iota(jnp.int32, named.shape, 2)
        scale = jnp.sum(jnp.where(lane == token, named, 0.0), axis=2, keepdims=True)
        scale = scale.reshape(groups * ROWS, 1)
        step = min(256, ff)
        rows = xn[...].reshape(groups * ROWS, 2 * half)
        for n in range(0, ff, step):
            gate_value = jnp.dot(rows, wg[:, n : n + step], preferred_element_type=jnp.float32)
            up_value = jnp.dot(rows, wu[:, n : n + step], preferred_element_type=jnp.float32)
            value = gate_value / (1.0 + jnp.exp(-gate_value)) * up_value * scale
            hidden[:, n : n + step] = value.astype(jnp.bfloat16)

    def stage_d(p):
        slot = p % DEPTH

        @pl.when(p >= DEPTH)
        def _():
            wait(d_send.at[p - DEPTH], part_o.at[slot])
            wait(e_send.at[p - DEPTH], part_m.at[slot, 0 : SIDE - 1])

        for at, part in ((1, part_o), (0, part_m)):
            value = jnp.dot(hidden[...], wd[at], preferred_element_type=jnp.float32)
            value = value.astype(jnp.bfloat16)
            for y_at in range(SIDE):
                for x_at in range(SIDE):
                    v_at, u_at = place(y_at, x_at)
                    top = (y_at * (SIDE // 2) + x_at // 2) * ROWS
                    left = x_at % 2 * block
                    part[slot, v_at, u_at] = value[top : top + ROWS, left : left + block]
            if at == 1:
                for k in (2, 1, 3, 0):
                    to = lax.rem(v + k, SIDE)
                    send(part_o.at[slot, to], rs1.at[slot, :, to], d_send.at[p], r1_recv.at[p, k],
                         z, sibling)

    def stage_e(p):
        slot = p % DEPTH
        for j in (2, 1, 3, 0):
            to = lax.rem(u + j, SIDE)
            wait(r1_recv.at[p, j], rs1.at[slot, :, to])
            for k in (2, 1, 3, 0):
                at = lax.rem(v + k, SIDE)
                value = part_m[slot, at, to].astype(jnp.float32) + rs1[slot, at, to].astype(jnp.float32)
                part_m[slot, at, to] = value.astype(jnp.bfloat16)
                if k:
                    send(part_m.at[slot, at, to], rs2.at[slot, k - 1, to], e_send.at[p],
                         r2_recv.at[p, j], z, dev(u, at))

    def stage_f(p):
        slot = p % DEPTH
        @pl.when(p >= DEPTH)
        def _():
            wait(f_send.at[p - DEPTH], fbuf.at[slot, 0 : SIDE - 1])

        for k in (2, 1, 3, 0):
            at = lax.rem(u + k, SIDE)
            wait(r2_recv.at[p, k], rs2.at[slot, :, at])
            value = part_m[slot, v, at].astype(jnp.float32)
            for j in range(SIDE - 1):
                value = value + rs2[slot, j, at].astype(jnp.float32)
            fbuf[slot, at] = value.astype(jnp.bfloat16)
            if k:
                send(fbuf.at[slot, at], rs3.at[p, k - 1], f_send.at[p], r3_recv.at[p],
                     z, dev(at, v))

    def stage_g(p):
        slot = p % DEPTH
        q = p // 4
        wait(r3_recv.at[p], rs3.at[p])
        value = xg[p, 0, v, u].astype(jnp.float32) + fbuf[slot, u].astype(jnp.float32)
        for j in range(SIDE - 1):
            value = value + rs3[p, j].astype(jnp.float32)
        obuf[p] = value.astype(jnp.bfloat16)

        @pl.when(z < planes - 1)
        def _():
            for k in (0, 1, 3, 2):
                send(obuf.at[p], xg.at[p, 0, v, u], g_send.at[p], x_recv.at[p, k],
                     z + 1, dev(lax.rem(u + k, SIDE), v))

        @pl.when(p % 4 == mine)
        def _():
            pltpu.make_async_copy(obuf.at[p], rows_of(out, q, mine), o_send.at[p]).start()

        @pl.when(p % 4 != mine)
        def _():
            send(obuf.at[p], rows_of(out, q, mine), o_send.at[p], o_recv.at[p], z, member(p % 4))

    inject(0)
    tell()
    inject(1)
    stage_h(0)

    stages = dict(a=stage_a, b=stage_b, n=stage_n, u=stage_u, d=stage_d, e=stage_e, f=stage_f, g=stage_g)
    ahead = max(lag for _, lag in ORDER)

    def iteration(i, _):
        @pl.when(i == LOADED)
        def _():
            for load in loads:
                load.wait()

        @pl.when(i % 4 == 0)
        def _():
            inject(i // 4 + 2)

        @pl.when(i + 1 < pieces)
        def _():
            stage_h(i + 1)

        for names, lag in ORDER:

            @pl.when((i >= lag) & (i - lag < pieces))
            def _(names=names, lag=lag):
                for name in names:
                    stages[name](i - lag)

        return 0

    lax.fori_loop(0, pieces + ahead, iteration, 0)

    def drain(p, _):
        wait(y_send.at[p], xg.at[p, 0, 0 : SIDE - 1])
        wait(s_send.at[p], xg.at[p, 0])

        @pl.when(p >= pieces - DEPTH)
        def _():
            wait(d_send.at[p], part_o.at[0])
            wait(e_send.at[p], part_m.at[0, 0 : SIDE - 1])
            wait(f_send.at[p], fbuf.at[0, 0 : SIDE - 1])

        @pl.when(z < planes - 1)
        def _():
            wait(g_send.at[p], xg.at[p, 0, v])

        wait(o_send.at[p], obuf.at[p])

        @pl.when(p % 4 == mine)
        def _():
            wait(o_recv.at[p], xg.at[p, 0, 0, 0 : SIDE - 1])

        @pl.when(z == 0)
        def _():
            wait(h_send.at[p], xg.at[p, 0, v, 0 : SIDE - 1])

        @pl.when((z == 0) & (p % 4 == mine))
        def _():
            wait(i_send.at[p // 4], xg.at[p, 0, 0, 0 : SIDE - 1])

        return 0

    lax.fori_loop(0, pieces, drain, 0)
    wait(t_send, told.at[0 : members - 1])


def on_device(
    activations, norm_gain, placement, expert_ids, expert_weights, gate_store, up_store, down_store
):
    planes = lax.axis_size("pipe")
    members = lax.axis_size("expert")
    micro, rows_local, width = activations.shape
    half, block = width // 2, width // 4
    ff = gate_store.shape[-1]
    rows = micro * rows_local
    depth = rows // ROWS
    pieces = 4 * depth
    total = SIDE * SIDE // 2 * ROWS
    bf16 = jnp.bfloat16
    ids = expert_ids.reshape(rows, -1).T
    weights = expert_weights.reshape(rows, -1).T

    dma = pltpu.SemaphoreType.DMA
    vmem = pl.BlockSpec(memory_space=pltpu.VMEM)
    smem = pl.BlockSpec(memory_space=pltpu.SMEM)
    hbm = pl.BlockSpec(memory_space=pl.ANY)
    out = pl.pallas_call(
        functools.partial(layer_kernel, planes, pieces),
        out_shape=jax.ShapeDtypeStruct((micro, rows_local, width), bf16),
        in_specs=[hbm, vmem, vmem, vmem, smem, hbm, hbm, hbm],
        out_specs=vmem,
        scratch_shapes=[
            pltpu.VMEM((1, width), jnp.float32),
            pltpu.VMEM((members, 8, rows), jnp.float32),
            pltpu.VMEM((4, SIDE * SIDE // 2, 8, rows), jnp.float32),
            pltpu.VMEM((width, ff), bf16),
            pltpu.VMEM((width, ff), bf16),
            pltpu.VMEM((2, ff, half), bf16),
            pltpu.VMEM((pieces, 2, SIDE, SIDE, ROWS, block), bf16),
            pltpu.VMEM((SIDE, SIDE // 2, ROWS, width), bf16),
            pltpu.VMEM((total, ff), bf16),
            pltpu.VMEM((DEPTH, SIDE, SIDE, ROWS, block), bf16),
            pltpu.VMEM((DEPTH, SIDE - 1, SIDE, ROWS, block), bf16),
            pltpu.VMEM((pieces, SIDE - 1, ROWS, block), bf16),
            pltpu.VMEM((DEPTH, SIDE, SIDE, ROWS, block), bf16),
            pltpu.VMEM((DEPTH, SIDE, SIDE, ROWS, block), bf16),
            pltpu.VMEM((DEPTH, SIDE, ROWS, block), bf16),
            pltpu.VMEM((pieces, ROWS, block), bf16),
            dma((6,)),
            dma,
            dma,
            dma((depth,)),
            dma((pieces,)),
            dma((pieces,)),
            dma((pieces, SIDE)),
            dma((pieces,)),
            dma((pieces, SIDE - 1)),
            *[dma((pieces,))] * 3,
            dma((pieces, SIDE)),
            dma((pieces,)),
            dma((pieces, SIDE)),
            *[dma((pieces,))] * 5,
        ],
        compiler_params=pltpu.CompilerParams(
            collective_id=0, has_side_effects=True, vmem_limit_bytes=60 * 2**20
        ),
        name="layers",
    )(activations, norm_gain.astype(jnp.float32), ids, weights, placement, gate_store, up_store, down_store)
    return out[None]


def solution(mesh):
    in_specs = (
        P(None, "expert", None),
        P("pipe", None),
        P("pipe", None),
        P("pipe", None, "expert", None),
        P("pipe", None, "expert", None),
        P("pipe", "expert", None, None),
        P("pipe", "expert", None, None),
        P("pipe", "expert", None, None),
    )
    out_specs = P("pipe", None, "expert", None)
    return jax.shard_map(
        on_device, mesh=mesh, in_specs=in_specs, out_specs=out_specs, check_vma=False
    )
```
